32 devices in a mesh: groups: 2 (over y), dp: 4 (over z), tensor: 4 (over x, core).
Axes of the slice: x: 2, y: 2, z: 4, core: 2. Of those that a mesh axis runs over, the one named last changes fastest.
Arguments:
- tokens: bfloat16 [6144, 8192], P(('groups', 'dp'), 'tensor'), parts along dimension 0, may hold values from -6 to 6
- value_weight_frozen: bfloat16 [8192, 1024], P('tensor'), may hold values from -0.0625 to 0.0625
- adapter_down_weight: bfloat16 [8192, 128], P('tensor', ('groups', 'dp')), parts along dimension 1, may hold values from -0.0625 to 0.0625
- adapter_up_weight: bfloat16 [1024, 128], P('tensor', ('groups', 'dp')), parts along dimension 1, may hold values from -1.5 to 1.5
- slot_adapter_index: int32 [6144], P(('groups', 'dp')), parts along dimension 0, may hold values from 0 to 3, never falling along the last dimension, each value on 1 to 1536 neighbouring positions
- adapter_owner_slot: int32 [8], P('groups'), parts along dimension 0, may hold values from 0 to 3, each once
- balanced_row_index: int32 [6144], P(('groups', 'dp')), parts along dimension 0, may hold values from -1 to 1535, as said below
- cotangent: bfloat16 [3072, 1024], P(('groups', 'dp'), 'tensor'), parts along dimension 0, may hold values from -0.119628906 to 0.119628906
Outputs:
- projected: bfloat16 [3072, 1024], P(('groups', 'dp'), 'tensor'), parts along dimension 0
- grad_down: float32 [8192, 128], P('tensor', ('groups', 'dp')), parts along dimension 1
- grad_up: float32 [1024, 128], P('tensor', ('groups', 'dp')), parts along dimension 1
The draws below stay inside these ranges and needn't reach their ends.
There are 2 independent parts, one for each index of `groups`. The reference program is written for one: setup_inputs(seed, part) draws one part's arguments, and reference() takes and returns one part's arrays. A program takes and returns all parts, laid end to end along the dimension named above; an argument that names none is the same for every part. Nothing has to cross between parts.
Inputs may be any that keep to these rules, and one draw needn't show every extreme that they name: `balanced_row_index`: each index of dp holds its live slots first and -1 after them; every balanced row 0 to 1535 is named by exactly one slot; the live slots of one index of dp name at most 192 rows of any one block of 384 balanced rows, and some index names exactly 192 rows of some block in every draw; some index of dp has all 768 slots live. `slot_adapter_index`: never falls along the token slots; each adapter holds 1 to 1536 slots, one exactly 1536. `adapter_owner_slot`: each owner slot exactly once.
All inputs are finite; a program needn't handle non-finite values.
Results may differ from the reference program's by a relative error of at most 0.0055.
Values may be sent and summed in bfloat16 or wider, within the bound.
A program may use at most 64 MiB of HBM per device.

```python
import math
import jax
import jax.numpy as jnp
import numpy as np
from jax import lax

MODEL_WIDTH = 8192
VALUE_FEATURES = 1024
ADAPTER_RANK = 16
TOK_DEV = 768
ADAPTER_TOTAL = 4
BAL = 384
UNIT = 96
TOKENS = 3072
TOTAL = 1536
N_DP = 4


def draw_balanced_row_index(key, part):
    key = jax.random.fold_in(key, 7)
    key_pair, key_shift, key_order = jax.random.split(key, 3)
    half_count = N_DP // 2
    pairing = jax.random.permutation(key_pair, N_DP)
    shifts = jax.random.randint(key_shift, (half_count,), 0, N_DP).astype(jnp.int32)
    shifts = shifts.at[0].set(N_DP)
    units = jnp.full((N_DP,), N_DP, jnp.int32)
    units = units.at[pairing[:half_count]].add(shifts)
    units = units.at[pairing[half_count:2 * half_count]].add(-shifts)
    order = jax.random.permutation(key_order, N_DP)
    position = jnp.zeros((N_DP,), jnp.int32).at[order].set(jnp.arange(N_DP, dtype=jnp.int32))
    before = (position[None, :] < position[:, None]).astype(jnp.int32)
    offsets = jnp.sum(before * units[None, :], axis=1)
    slot_range = jnp.arange(TOKENS, dtype=jnp.int32)
    device = slot_range // TOK_DEV
    inner = slot_range % TOK_DEV
    unit_index = offsets[device] + inner // UNIT
    is_live = inner < units[device] * UNIT
    target = unit_index % N_DP
    result = target * BAL + unit_index // N_DP * UNIT + inner % UNIT
    return jnp.where(is_live, result, -1).astype(jnp.int32)


def block_scale(stream_key, extent, cuts, low, high):
    factor_of, own = 1.0, jax.random.fold_in(stream_key, 6)
    for axis_at, shards_of in cuts:
        steps = jnp.exp(jax.random.uniform(jax.random.fold_in(own, axis_at), (shards_of,), jnp.float32, low / len(cuts), high / len(cuts)))
        factor_of = factor_of * jnp.repeat(steps, extent[axis_at] // shards_of).reshape([-1 if axis == axis_at else 1 for axis in range(len(extent))])
    return factor_of


def profile(count, total, limit, lean):
    weights = [(1 << 20) // math.isqrt(standing ** lean) + 1 for standing in range(2, count + 1)]
    spare, holding = total - limit - (count - 1), [1] * (count - 1)
    while spare > 0:
        candidates = [i for i in range(count - 1) if holding[i] < limit]
        pool, remaining = sum([weights[i] for i in candidates]), spare
        for i in candidates:
            more = min(limit - holding[i], max(1, remaining * weights[i] // pool), spare)
            holding[i] = holding[i] + more
            spare = spare - more
    return np.array([limit] + holding)


def uneven_parts(rng, count, total, limit, lean):
    if count == 2:
        one = jax.random.randint(rng, (), max(1, total - limit), min(limit, total - 1) + 1)
        return jnp.stack([one, total - one])
    lengths = jnp.asarray(profile(count, total, limit, lean), jnp.int32)
    twos = (count - 1) // 2
    donor, taker = lengths[1:1 + 2 * twos:2], lengths[2:2 + 2 * twos:2]
    room = jnp.minimum(donor - 1, limit - taker)
    moved = jax.random.randint(jax.random.fold_in(rng, 1), (twos,), 0, 1 << 20) % (room + 1)
    lengths = lengths.at[1:1 + 2 * twos:2].set(donor - moved).at[2:2 + 2 * twos:2].set(taker + moved)
    return lengths[jax.random.permutation(jax.random.fold_in(rng, 2), count)]


def bell_draw(rng, extent, deviation, reach, pieces=(), held_as=jnp.bfloat16):
    entries = deviation * jax.random.normal(rng, extent, jnp.float32)
    if pieces:
        entries = entries * block_scale(rng, extent, pieces, -0.22, 0.18)
    return jnp.clip(entries, -reach, reach).astype(held_as)


def setup_inputs(seed: int = 0, part: int = 0) -> dict:
    seeds = jax.random.split(jax.random.key(seed), 9)
    own_keys = jax.random.split(jax.random.fold_in(seeds[8], part), 9)
    return {
        "tokens": bell_draw(own_keys[0], (TOKENS, MODEL_WIDTH), 1.0, 6.0, ((0, 4), (1, 4))),
        "value_weight_frozen": bell_draw(seeds[1], (MODEL_WIDTH, VALUE_FEATURES), MODEL_WIDTH ** -0.5, 0.0625, ((0, 4),)),
        "adapter_down_weight": bell_draw(own_keys[2], (MODEL_WIDTH, ADAPTER_TOTAL * ADAPTER_RANK), MODEL_WIDTH ** -0.5, 0.0625, ((0, 4), (1, 4))),
        "adapter_up_weight": bell_draw(own_keys[3], (VALUE_FEATURES, ADAPTER_TOTAL * ADAPTER_RANK), ADAPTER_RANK ** -0.5, 1.5, ((0, 4), (1, 4))),
        "slot_adapter_index": jnp.searchsorted(jnp.cumsum(uneven_parts(own_keys[4], ADAPTER_TOTAL, TOKENS, 2 * TOK_DEV, 2)), jnp.arange(TOKENS), side="right").astype(jnp.int32),
        "adapter_owner_slot": jax.random.permutation(own_keys[5], ADAPTER_TOTAL).astype(jnp.int32),
        "balanced_row_index": draw_balanced_row_index(jax.random.fold_in(jax.random.fold_in(seeds[8], part), 71), part),
        "cotangent": bell_draw(own_keys[7], (TOTAL, VALUE_FEATURES), 0.02, 0.119628906, ((0, 4), (1, 4))),
    }


SCALE = 2.0


def reference(tokens, value_weight_frozen, adapter_down_weight, adapter_up_weight, slot_adapter_index, adapter_owner_slot, balanced_row_index, cotangent):
    slot_total = cotangent.shape[0]
    adapters = adapter_owner_slot.shape[0]
    owner = adapter_owner_slot[slot_adapter_index].astype(jnp.int32)
    dest_index = jnp.where(balanced_row_index >= 0, balanced_row_index, slot_total).astype(jnp.int32)
    source = jnp.zeros((slot_total,), jnp.int32).at[dest_index].set(jnp.arange(tokens.shape[0], dtype=jnp.int32), mode="drop")
    rows_bal = tokens[source].reshape(N_DP, BAL, MODEL_WIDTH)
    owner_bal = owner[source].reshape(N_DP, BAL)
    cot_bal = cotangent.reshape(N_DP, BAL, VALUE_FEATURES)
    up_weight_wide = adapter_up_weight.astype(jnp.float32)
    adapter_range = jnp.arange(adapters, dtype=jnp.int32)

    def one_block(totals, block_items):
        token_rows_block, owner_blk, cotangent_block = block_items
        onehot = (owner_blk[:, None] == adapter_range[None, :]).astype(jnp.float32)
        down_projected = jnp.dot(token_rows_block, adapter_down_weight, preferred_element_type=jnp.float32)
        low_rank = jnp.sum(down_projected.reshape(BAL, adapters, ADAPTER_RANK) * onehot[:, :, None], axis=1)
        base_part = jnp.dot(token_rows_block, value_weight_frozen, preferred_element_type=jnp.float32)
        low_wide = (onehot[:, :, None] * low_rank[:, None, :]).reshape(BAL, adapters * ADAPTER_RANK)
        lifted = jnp.dot(low_wide, up_weight_wide.T, precision=lax.Precision.HIGHEST)
        out_rows = (base_part + SCALE * lifted).astype(jnp.bfloat16)
        cotangent_projected = jnp.dot(cotangent_block, adapter_up_weight, preferred_element_type=jnp.float32)
        grad_low = jnp.sum(cotangent_projected.reshape(BAL, adapters, ADAPTER_RANK) * onehot[:, :, None], axis=1)
        mask_half = onehot.astype(jnp.bfloat16)
        grad_spread = (mask_half[:, :, None] * grad_low.astype(jnp.bfloat16)[:, None, :]).reshape(BAL, adapters * ADAPTER_RANK)
        low_spread = (mask_half[:, :, None] * low_rank.astype(jnp.bfloat16)[:, None, :]).reshape(BAL, adapters * ADAPTER_RANK)
        down_term = SCALE * jnp.dot(token_rows_block.T, grad_spread, preferred_element_type=jnp.float32)
        up_term = SCALE * jnp.dot(cotangent_block.T, low_spread, preferred_element_type=jnp.float32)
        return (totals[0] + down_term, totals[1] + up_term), out_rows

    start = (jnp.zeros((MODEL_WIDTH, adapters * ADAPTER_RANK), jnp.float32), jnp.zeros((VALUE_FEATURES, adapters * ADAPTER_RANK), jnp.float32))
    sums, outputs = lax.scan(one_block, start, (rows_bal, owner_bal, cot_bal))
    return outputs.reshape(slot_total, VALUE_FEATURES), sums[0], sums[1]
```

```python
import functools

import jax
import jax.numpy as jnp
from jax import lax
from jax.experimental import pallas as pl
from jax.experimental.pallas import tpu as pltpu
from jax.sharding import PartitionSpec as P

SCALE = 2.0
RANK = 16
F32 = jnp.float32
BF16 = jnp.bfloat16
MESH = pl.DeviceIdType.MESH

NN = (((1,), (0,)), ((), ()))
NT = (((1,), (1,)), ((), ()))
TN = (((0,), (0,)), ((), ()))


def mm(a, b, dims=NN):
    return lax.dot_general(a, b, dims, preferred_element_type=F32)


def onehot(cond):
    return jnp.where(cond, 1.0, 0.0).astype(BF16)


def kernel(
    n, T, G, adapters,
    slot_ref, tok_hbm, w_hbm, fac_ref, sidx_ref, bidx_ref, cot_ref,
    out_ref, grad_ref,
    tok, w, rows, fac_all, cot_all, cotb,
    sib_send, sib_recv, own, x_send, x_recv,
    low_send, low_recv, gl_send, gl_recv,
    z_send, z_recv, zm_send, zm_recv, g_send, g_recv,
    local_sem, fac_ss, fac_rs, cot_ss, cot_rs, sib_ss, sib_rs, x_ss, x_rs,
    low_ss, low_rs, gl_ss, gl_rs, z_ss, z_rs, zm_ss, zm_rs, g_ss, g_rs,
):
    me = lax.axis_index("dp")
    q = lax.axis_index("tensor")
    slots, depth = tok.shape
    bal, vw = out_ref.shape
    cap = z_send.shape[1]
    H = T // 2
    per = n // G
    chunk = per * cap
    half = q // 2
    parity = lax.rem(q, 2)

    def peer_dp(k):
        return lax.rem(me + k, n)

    def peer_t(k):
        return lax.rem(q + k, T)

    loads = [pltpu.make_async_copy(tok_hbm, tok, local_sem.at[T])]
    for k in range(H):
        for own_side in range(2):
            par = parity if own_side else 1 - parity
            block = 2 * lax.rem(half + k, H) + par
            loads.append(
                pltpu.make_async_copy(
                    w_hbm.at[:, pl.ds(pl.multiple_of(block * vw, vw), vw)],
                    w.at[own_side * H + k],
                    local_sem.at[own_side * H + k],
                )
            )
    for c in loads:
        c.start()

    barrier = pltpu.get_barrier_semaphore()
    for k in range(1, n):
        pl.semaphore_signal(barrier, inc=1, device_id={"dp": peer_dp(k)}, device_id_type=MESH)
    for k in range(1, T):
        pl.semaphore_signal(barrier, inc=1, device_id={"tensor": peer_t(k)}, device_id_type=MESH)
    fac_all[me] = fac_ref[...]
    cot_all[me] = cot_ref[...]
    pl.semaphore_wait(barrier, n - 1 + T - 1)

    def line(buf, ss, rs):
        def send(k):
            for way in range(2):
                if way == 0:
                    block, to = me - k + 1, me + 1
                    ok = jnp.logical_and(block >= 0, to < n)
                else:
                    block, to = me + k - 1, me - 1
                    ok = jnp.logical_and(block < n, to >= 0)
                at = jnp.clip(block, 0, n - 1)
                tgt = jnp.clip(to, 0, n - 1)

                @pl.when(ok)
                def _():
                    pltpu.make_async_remote_copy(
                        src_ref=buf.at[at], dst_ref=buf.at[at],
                        send_sem=ss.at[way, k - 1], recv_sem=rs.at[way, k - 1],
                        device_id={"dp": tgt}, device_id_type=MESH,
                    ).start()

        def finish(k, sending):
            for way in range(2):
                if sending:
                    block = me - k + 1 if way == 0 else me + k - 1
                    to = me + 1 if way == 0 else me - 1
                    ok = jnp.logical_and(
                        jnp.logical_and(block >= 0, block < n),
                        jnp.logical_and(to >= 0, to < n),
                    )
                else:
                    block = me - k if way == 0 else me + k
                    ok = jnp.logical_and(block >= 0, block < n)
                at = jnp.clip(block, 0, n - 1)
                tgt = jnp.where(me > 0, me - 1, me + 1)

                @pl.when(ok)
                def _():
                    c = pltpu.make_async_remote_copy(
                        src_ref=buf.at[at], dst_ref=buf.at[at],
                        send_sem=ss.at[way, k - 1], recv_sem=rs.at[way, k - 1],
                        device_id={"dp": tgt}, device_id_type=MESH,
                    )
                    if sending:
                        c.wait_send()
                    else:
                        c.wait_recv()

        def advance(k):
            finish(k, False)
            if k < n - 1:
                send(k + 1)

        return send, finish, advance

    fac_step, fac_finish, fac_advance = line(fac_all, fac_ss, fac_rs)
    cot_step, cot_finish, cot_advance = line(cot_all, cot_ss, cot_rs)
    fac_step(1)
    cot_step(1)

    npad = max(16, n)
    bidx = bidx_ref[...]
    kio = lax.broadcasted_iota(jnp.int32, (npad, slots), 0)
    dest = lax.rem(me + 1 + kio, n)
    first = jnp.where(kio < n, dest * bal, 1 << 24)
    hit = jnp.logical_and(bidx >= first, bidx < first + bal)
    tri = onehot(
        lax.broadcasted_iota(jnp.int32, (slots, slots), 0)
        < lax.broadcasted_iota(jnp.int32, (slots, slots), 1)
    )
    rank = mm(onehot(hit), tri)
    place = jnp.where(hit, rank, -1.0)
    loc1 = jnp.sum(jnp.where(hit, bidx - first + 1, 0), axis=0, keepdims=True)
    sidx = sidx_ref[...]
    owner1 = jnp.zeros((1, slots), jnp.int32)
    for a in range(adapters):
        owner1 = jnp.where(sidx == a, slot_ref[a] + 1, owner1)
    rio = lax.broadcasted_iota(jnp.int32, (16, slots), 0)
    meta = jnp.where(
        rio == 0, loc1 >> 4, jnp.where(rio == 1, loc1 & 15, jnp.where(rio == 2, owner1, 0))
    ).astype(F32).astype(BF16)

    iota_cap = lax.broadcasted_iota(jnp.int32, (cap, slots), 0).astype(F32)
    loc_cols, own_rows = [], []

    def sib_copy(g):
        return pltpu.make_async_remote_copy(
            src_ref=sib_send.at[g], dst_ref=sib_recv.at[g],
            send_sem=sib_ss.at[g], recv_sem=sib_rs.at[g],
            device_id={"tensor": q + 1 - 2 * parity}, device_id_type=MESH,
        )

    def x_copy(g, k):
        return pltpu.make_async_remote_copy(
            src_ref=x_send.at[g, k - 1], dst_ref=x_recv.at[g, k - 1],
            send_sem=x_ss.at[g, k - 1], recv_sem=x_rs.at[g, k - 1],
            device_id={"tensor": 2 * lax.rem(half + k, H) + parity}, device_id_type=MESH,
        )

    def sum_pair(g):
        sib_copy(g).wait_recv()
        for k in list(range(1, H)) + [0]:
            total = own[g, k] + sib_recv[g, k].astype(F32)
            if k == 0:
                own[g, 0] = total
            else:
                x_send[g, k - 1] = total.astype(BF16)
                x_copy(g, k).start()

    steps = [k for k in range(1, n)]
    for g in range(G):
        parts = []
        for k in range(g * per, (g + 1) * per):
            b = onehot(iota_cap == place[k:k + 1, :])
            parts.append(b)
            row = mm(meta, b, NT)
            zm_send[k] = jnp.broadcast_to(row[0:1] * 16.0 + row[1:2], (8, cap))
            col = mm(b, meta, NT)
            loc_cols.append(col[:, 0:1] * 16.0 + col[:, 1:2])
        bg = parts[0] if per == 1 else jnp.concatenate(parts, axis=0)
        own_rows.append(mm(meta, bg, NT)[2:3] - 1.0)
        if g == 0:
            loads[0].wait()
        rows[g] = mm(bg, tok[...]).astype(BF16)
        for k in range(H):
            if g == 0:
                loads[1 + 2 * k].wait()
            sib_send[g, k] = mm(rows[g], w[k]).astype(BF16)
        sib_copy(g).start()
        for k in range(H):
            if g == 0:
                loads[2 + 2 * k].wait()
            own[g, k] = mm(rows[g], w[H + k])
        if g > 0:
            sum_pair(g - 1)
        for k in steps[g * (n - 1) // G:(g + 1) * (n - 1) // G]:
            fac_advance(k)
            cot_advance(k)

    def select(dense, g):
        total = jnp.zeros((RANK, chunk), F32)
        for p in range(n):
            total = total + jnp.where(
                own_rows[g] == float(p), dense[p * RANK:(p + 1) * RANK, :], 0.0
            )
        return total

    def spread(values, g):
        return jnp.concatenate(
            [jnp.where(own_rows[g] == float(p), values, 0.0) for p in range(n)], axis=0
        )

    def low_copy(k, send, recv, ss, rs):
        return pltpu.make_async_remote_copy(
            src_ref=send, dst_ref=recv.at[k - 1],
            send_sem=ss.at[k - 1], recv_sem=rs.at[k - 1],
            device_id={"tensor": peer_t(k)}, device_id_type=MESH,
        )

    down = fac_all[:, :, :depth].reshape(n * RANK, depth)
    up = fac_all[:, :, depth:].reshape(n * RANK, vw)
    for g in range(G):
        low_send[g] = select(mm(down, rows[g], NT), g)
    for k in range(1, T):
        low_copy(k, low_send, low_recv, low_ss, low_rs).start()
    sum_pair(G - 1)

    for g in range(G):
        for i in range(per):
            k = g * per + i
            col = loc_cols[k]
            pick = onehot(
                col == (lax.broadcasted_iota(jnp.int32, (cap, bal), 1) + 1).astype(F32)
            )
            cotb[g, i * cap:(i + 1) * cap, :] = mm(pick, cot_all[peer_dp(k + 1)]).astype(BF16)
        gl_send[g] = select(mm(up, cotb[g], NT), g)
    for k in range(1, T):
        low_copy(k, gl_send, gl_recv, gl_ss, gl_rs).start()

    def z_copy(k, send, recv, ss, rs):
        return pltpu.make_async_remote_copy(
            src_ref=send.at[k], dst_ref=recv.at[k],
            send_sem=ss.at[k], recv_sem=rs.at[k],
            device_id={"dp": peer_dp(k + 1)}, device_id_type=MESH,
        )

    for k in range(n - 1):
        z_copy(k, zm_send, zm_recv, zm_ss, zm_rs).start()

    for k in range(1, T):
        low_copy(k, low_send, low_recv, low_ss, low_rs).wait_recv()
    up_twice = jnp.concatenate([up, up], axis=0)
    low_spreads = []
    for g in range(G):
        low = low_send[g]
        for k in range(T - 1):
            low = low + low_recv[k, g]
        high = low.astype(BF16)
        rest = low - high.astype(F32)
        high_s = spread(high.astype(F32), g).astype(BF16)
        low_spreads.append(high_s)
        both = jnp.concatenate([high_s, spread(rest, g).astype(BF16)], axis=0)
        total = own[g, 0] + SCALE * mm(both, up_twice, TN)
        for k in range(1, H):
            x_copy(g, k).wait_recv()
            total = total + x_recv[g, k - 1].astype(F32)
        done = total.astype(BF16)
        for i in range(per):
            k = g * per + i
            z_send[k] = done[i * cap:(i + 1) * cap, :]
            if k < n - 1:
                z_copy(k, z_send, z_recv, z_ss, z_rs).start()

    for k in range(1, T):
        low_copy(k, gl_send, gl_recv, gl_ss, gl_rs).wait_recv()
    d_down = jnp.zeros((n * RANK, depth), F32)
    d_up = jnp.zeros((n * RANK, vw), F32)
    for g in range(G):
        gl = gl_send[g]
        for k in range(T - 1):
            gl = gl + gl_recv[k, g]
        gl_s = spread(gl.astype(BF16).astype(F32), g).astype(BF16)
        d_down = d_down + mm(gl_s, rows[g])
        d_up = d_up + mm(low_spreads[g], cotb[g])
    g_send[:, :, :depth] = (SCALE * d_down).astype(BF16).reshape(n, RANK, depth)
    g_send[:, :, depth:] = (SCALE * d_up).astype(BF16).reshape(n, RANK, vw)

    def g_copy(k):
        return pltpu.make_async_remote_copy(
            src_ref=g_send.at[peer_dp(k)], dst_ref=g_recv.at[k - 1],
            send_sem=g_ss.at[k - 1], recv_sem=g_rs.at[k - 1],
            device_id={"dp": peer_dp(k)}, device_id_type=MESH,
        )

    for k in range(1, n):
        g_copy(k).start()

    jio = (lax.broadcasted_iota(jnp.int32, (bal, cap), 0) + 1).astype(F32)
    result = mm(onehot(zm_send[n - 1][0:1] == jio), z_send[n - 1])
    for k in range(n - 1):
        z_copy(k, zm_send, zm_recv, zm_ss, zm_rs).wait_recv()
        z_copy(k, z_send, z_recv, z_ss, z_rs).wait_recv()
        result = result + mm(onehot(zm_recv[k][0:1] == jio), z_recv[k])
    out_ref[...] = result.astype(BF16)

    total = g_send[me].astype(F32)
    for k in range(1, n):
        g_copy(k).wait_recv()
        total = total + g_recv[k - 1].astype(F32)
    grad_ref[...] = total

    for k in range(1, n):
        fac_finish(k, True)
        cot_finish(k, True)
        g_copy(k).wait_send()
        z_copy(k - 1, zm_send, zm_recv, zm_ss, zm_rs).wait_send()
        z_copy(k - 1, z_send, z_recv, z_ss, z_rs).wait_send()
    for g in range(G):
        sib_copy(g).wait_send()
        for k in range(1, H):
            x_copy(g, k).wait_send()
    for k in range(1, T):
        low_copy(k, low_send, low_recv, low_ss, low_rs).wait_send()
        low_copy(k, gl_send, gl_recv, gl_ss, gl_rs).wait_send()


def body(n, T, tokens, weight, down, up, slot_adapter, owner_slot, balanced, cotangent):
    slots, depth = tokens.shape
    bal, vw = cotangent.shape
    adapters = owner_slot.shape[0]
    cap = -(-(slots // n) // 16) * 16
    G = 4 if n % 4 == 0 else n
    chunk = n // G * cap
    H = T // 2
    factors = jnp.concatenate([down.T, up.T], axis=1)
    vmem, hbm = pl.BlockSpec(memory_space=pltpu.VMEM), pl.BlockSpec(memory_space=pl.ANY)
    dma = pltpu.SemaphoreType.DMA
    projected, grads = pl.pallas_call(
        functools.partial(kernel, n, T, G, adapters),
        out_shape=(
            jax.ShapeDtypeStruct((bal, vw), BF16),
            jax.ShapeDtypeStruct((RANK, depth + vw), F32),
        ),
        in_specs=[pl.BlockSpec(memory_space=pltpu.SMEM), hbm, hbm, vmem, vmem, vmem, vmem],
        out_specs=(vmem, vmem),
        scratch_shapes=[
            pltpu.VMEM((slots, depth), BF16),
            pltpu.VMEM((T, depth, vw), BF16),
            pltpu.VMEM((G, chunk, depth), BF16),
            pltpu.VMEM((n, RANK, depth + vw), BF16),
            pltpu.VMEM((n, bal, vw), BF16),
            pltpu.VMEM((G, chunk, vw), BF16),
            pltpu.VMEM((G, H, chunk, vw), BF16),
            pltpu.VMEM((G, H, chunk, vw), BF16),
            pltpu.VMEM((G, H, chunk, vw), F32),
            pltpu.VMEM((G, H - 1, chunk, vw), BF16),
            pltpu.VMEM((G, H - 1, chunk, vw), BF16),
            pltpu.VMEM((G, RANK, chunk), F32),
            pltpu.VMEM((T - 1, G, RANK, chunk), F32),
            pltpu.VMEM((G, RANK, chunk), F32),
            pltpu.VMEM((T - 1, G, RANK, chunk), F32),
            pltpu.VMEM((n, cap, vw), BF16),
            pltpu.VMEM((n, cap, vw), BF16),
            pltpu.VMEM((n, 8, cap), F32),
            pltpu.VMEM((n, 8, cap), F32),
            pltpu.VMEM((n, RANK, depth + vw), BF16),
            pltpu.VMEM((n, RANK, depth + vw), BF16),
            dma((T + 1,)),
            dma((2, n - 1)), dma((2, n - 1)), dma((2, n - 1)), dma((2, n - 1)),
            dma((G,)), dma((G,)), dma((G, H - 1)), dma((G, H - 1)),
            dma((T - 1,)), dma((T - 1,)), dma((T - 1,)), dma((T - 1,)),
            dma((n - 1,)), dma((n - 1,)), dma((n - 1,)), dma((n - 1,)),
            dma((n - 1,)), dma((n - 1,)),
        ],
        compiler_params=pltpu.CompilerParams(
            collective_id=0, has_side_effects=True, vmem_limit_bytes=48 * 1024 * 1024
        ),
        name="value_lora",
    )(
        owner_slot, tokens, weight, factors,
        slot_adapter.reshape(1, slots), balanced.reshape(1, slots), cotangent,
    )
    return projected, grads[:, :depth].T, grads[:, depth:].T


def solution(mesh):
    rows = ("groups", "dp")
    return jax.shard_map(
        functools.partial(body, mesh.shape["dp"], mesh.shape["tensor"]),
        mesh=mesh,
        in_specs=(
            P(rows, "tensor"), P("tensor", None), P("tensor", rows), P("tensor", rows),
            P(rows), P("groups"), P(rows), P(rows, "tensor"),
        ),
        out_specs=(P(rows, "tensor"), P("tensor", rows), P("tensor", rows)),
        check_vma=False,
    )
```

```python
import functools

import jax
import jax.numpy as jnp
from jax import lax
from jax.experimental import pallas as pl
from jax.experimental.pallas import tpu as pltpu
from jax.sharding import PartitionSpec as P

SCALE = 2.0
RANK = 16
F32 = jnp.float32
BF16 = jnp.bfloat16
MESH = pl.DeviceIdType.MESH

NN = (((1,), (0,)), ((), ()))
NT = (((1,), (1,)), ((), ()))
TN = (((0,), (0,)), ((), ()))


def mm(a, b, dims=NN):
    return lax.dot_general(a, b, dims, preferred_element_type=F32)


def onehot(cond):
    return jnp.where(cond, 1.0, 0.0).astype(BF16)


def kernel(
    n, T, G, adapters,
    slot_hbm, tok_hbm, w_hbm, down_hbm, up_hbm, sidx_hbm, bidx_hbm, cot_hbm,
    out_ref, down_out, up_out,
    slot_ref, sidx_ref, bidx_ref, tok, w, rows, fac_all, cot_all, cotb,
    sib_send, sib_recv, own, x_send, x_recv,
    low_send, low_recv, gl_send, gl_recv,
    z_send, z_recv, zm_send, zm_recv, g_send, g_recv,
    small_sem, local_sem, fac_ss, fac_rs, cot_ss, cot_rs, sib_ss, sib_rs, x_ss, x_rs,
    low_ss, low_rs, gl_ss, gl_rs, z_ss, z_rs, zm_ss, zm_rs, g_ss, g_rs,
):
    me = lax.axis_index("dp")
    q = lax.axis_index("tensor")
    slots, depth = tok.shape
    bal, vw = out_ref.shape
    cap = z_send.shape[1]
    H = T // 2
    per = n // G
    chunk = per * cap
    half = q // 2
    parity = lax.rem(q, 2)

    def peer_dp(k):
        return lax.rem(me + k, n)

    def peer_t(k):
        return lax.rem(q + k, T)

    small = [
        pltpu.make_async_copy(src, dst, small_sem.at[i])
        for i, (src, dst) in enumerate((
            (down_hbm, fac_all.at[me, :, pl.ds(0, depth)]),
            (up_hbm, fac_all.at[me, :, pl.ds(depth, vw)]),
            (slot_hbm, slot_ref),
            (sidx_hbm, sidx_ref),
            (bidx_hbm, bidx_ref),
            (cot_hbm, cot_all.at[me]),
        ))
    ]
    for c in small:
        c.start()
    loads = [pltpu.make_async_copy(tok_hbm, tok, local_sem.at[T])]
    for k in range(H):
        for own_side in range(2):
            par = parity if own_side else 1 - parity
            block = 2 * lax.rem(half + k, H) + par
            loads.append(
                pltpu.make_async_copy(
                    w_hbm.at[:, pl.ds(pl.multiple_of(block * vw, vw), vw)],
                    w.at[own_side * H + k],
                    local_sem.at[own_side * H + k],
                )
            )
    for c in loads:
        c.start()

    barrier = pltpu.get_barrier_semaphore()
    for k in range(1, n):
        pl.semaphore_signal(barrier, inc=1, device_id={"dp": peer_dp(k)}, device_id_type=MESH)
    for k in range(1, T):
        pl.semaphore_signal(barrier, inc=1, device_id={"tensor": peer_t(k)}, device_id_type=MESH)
    pl.semaphore_wait(barrier, n - 1 + T - 1)

    def line(buf, ss, rs):
        def send(k):
            for way in range(2):
                if way == 0:
                    block, to = me - k + 1, me + 1
                    ok = jnp.logical_and(block >= 0, to < n)
                else:
                    block, to = me + k - 1, me - 1
                    ok = jnp.logical_and(block < n, to >= 0)
                at = jnp.clip(block, 0, n - 1)
                tgt = jnp.clip(to, 0, n - 1)

                @pl.when(ok)
                def _():
                    pltpu.make_async_remote_copy(
                        src_ref=buf.at[at], dst_ref=buf.at[at],
                        send_sem=ss.at[way, k - 1], recv_sem=rs.at[way, k - 1],
                        device_id={"dp": tgt}, device_id_type=MESH,
                    ).start()

        def finish(k, sending):
            for way in range(2):
                if sending:
                    block = me - k + 1 if way == 0 else me + k - 1
                    to = me + 1 if way == 0 else me - 1
                    ok = jnp.logical_and(
                        jnp.logical_and(block >= 0, block < n),
                        jnp.logical_and(to >= 0, to < n),
                    )
                else:
                    block = me - k if way == 0 else me + k
                    ok = jnp.logical_and(block >= 0, block < n)
                at = jnp.clip(block, 0, n - 1)
                tgt = jnp.where(me > 0, me - 1, me + 1)

                @pl.when(ok)
                def _():
                    c = pltpu.make_async_remote_copy(
                        src_ref=buf.at[at], dst_ref=buf.at[at],
                        send_sem=ss.at[way, k - 1], recv_sem=rs.at[way, k - 1],
                        device_id={"dp": tgt}, device_id_type=MESH,
                    )
                    if sending:
                        c.wait_send()
                    else:
                        c.wait_recv()

        def advance(k):
            finish(k, False)
            if k < n - 1:
                send(k + 1)

        return send, finish, advance

    fac_step, fac_finish, fac_advance = line(fac_all, fac_ss, fac_rs)
    cot_step, cot_finish, cot_advance = line(cot_all, cot_ss, cot_rs)
    small[0].wait()
    small[1].wait()
    fac_step(1)
    for c in small[2:]:
        c.wait()

    def row_of(ref):
        return jnp.concatenate([ref[i:i + 1, :] for i in range(ref.shape[0])], axis=1)

    npad = max(16, n)
    bidx = row_of(bidx_ref)
    kio = lax.broadcasted_iota(jnp.int32, (npad, slots), 0)
    dest = lax.rem(me + 1 + kio, n)
    first = jnp.where(kio < n, dest * bal, 1 << 24)
    hit = jnp.logical_and(bidx >= first, bidx < first + bal)
    tri = onehot(
        lax.broadcasted_iota(jnp.int32, (slots, slots), 0)
        < lax.broadcasted_iota(jnp.int32, (slots, slots), 1)
    )
    rank = mm(onehot(hit), tri)
    place = jnp.where(hit, rank, -1.0)
    loc1 = jnp.sum(jnp.where(hit, bidx - first + 1, 0), axis=0, keepdims=True)
    sidx = row_of(sidx_ref)
    owner1 = jnp.zeros((1, slots), jnp.int32)
    for a in range(adapters):
        owner1 = jnp.where(sidx == a, slot_ref[a] + 1, owner1)
    rio = lax.broadcasted_iota(jnp.int32, (16, slots), 0)
    meta = jnp.where(
        rio == 0, loc1 >> 4, jnp.where(rio == 1, loc1 & 15, jnp.where(rio == 2, owner1, 0))
    ).astype(F32).astype(BF16)

    iota_cap = lax.broadcasted_iota(jnp.int32, (cap, slots), 0).astype(F32)
    loc_cols, own_rows = [], []

    def sib_copy(g):
        return pltpu.make_async_remote_copy(
            src_ref=sib_send.at[g], dst_ref=sib_recv.at[g],
            send_sem=sib_ss.at[g], recv_sem=sib_rs.at[g],
            device_id={"tensor": q + 1 - 2 * parity}, device_id_type=MESH,
        )

    def x_copy(g, k):
        return pltpu.make_async_remote_copy(
            src_ref=x_send.at[g, k - 1], dst_ref=x_recv.at[g, k - 1],
            send_sem=x_ss.at[g, k - 1], recv_sem=x_rs.at[g, k - 1],
            device_id={"tensor": 2 * lax.rem(half + k, H) + parity}, device_id_type=MESH,
        )

    def sum_pair(g):
        sib_copy(g).wait_recv()
        for k in list(range(1, H)) + [0]:
            total = own[g, k] + sib_recv[g, k].astype(F32)
            if k == 0:
                own[g, 0] = total
            else:
                x_send[g, k - 1] = total.astype(BF16)
                x_copy(g, k).start()

    hops = [functools.partial(fac_advance, k) for k in range(1, n)]
    hops[0]()
    cot_step(1)
    share = -(-(n - 2) // max(1, G - 1))
    hops = hops[1:]
    for g in range(G):
        parts = []
        for k in range(g * per, (g + 1) * per):
            b = onehot(iota_cap == place[k:k + 1, :])
            parts.append(b)
            row = mm(meta, b, NT)
            zm_send[k] = jnp.broadcast_to(row[0:1] * 16.0 + row[1:2], (8, cap))
            col = mm(b, meta, NT)
            loc_cols.append(col[:, 0:1] * 16.0 + col[:, 1:2])
        bg = parts[0] if per == 1 else jnp.concatenate(parts, axis=0)
        own_rows.append(mm(meta, bg, NT)[2:3] - 1.0)
        if g == 0:
            loads[0].wait()
        rows[g] = mm(bg, tok[...]).astype(BF16)
        for k in range(H):
            if g == 0:
                loads[1 + 2 * k].wait()
            sib_send[g, k] = mm(rows[g], w[k]).astype(BF16)
        sib_copy(g).start()
        for k in range(H):
            if g == 0:
                loads[2 + 2 * k].wait()
            own[g, k] = mm(rows[g], w[H + k])
        if g > 0:
            sum_pair(g - 1)
        for hop in hops[g * share:(g + 1) * share]:
            hop()
        if g == G - 2:
            cot_advance(1)

    def select(dense, g):
        total = jnp.zeros((RANK, chunk), F32)
        for p in range(n):
            total = total + jnp.where(
                own_rows[g] == float(p), dense[p * RANK:(p + 1) * RANK, :], 0.0
            )
        return total

    def spread(values, g):
        return jnp.concatenate(
            [jnp.where(own_rows[g] == float(p), values, 0.0) for p in range(n)], axis=0
        )

    def low_copy(k, send, recv, ss, rs):
        return pltpu.make_async_remote_copy(
            src_ref=send, dst_ref=recv.at[k - 1],
            send_sem=ss.at[k - 1], recv_sem=rs.at[k - 1],
            device_id={"tensor": peer_t(k)}, device_id_type=MESH,
        )

    down = fac_all[:, :, :depth].reshape(n * RANK, depth)
    up = fac_all[:, :, depth:].reshape(n * RANK, vw)
    for g in range(G):
        low_send[g] = select(mm(down, rows[g], NT), g)
    for k in range(1, T):
        low_copy(k, low_send, low_recv, low_ss, low_rs).start()
    sum_pair(G - 1)

    def z_copy(k, send, recv, ss, rs):
        return pltpu.make_async_remote_copy(
            src_ref=send.at[k], dst_ref=recv.at[k],
            send_sem=ss.at[k], recv_sem=rs.at[k],
            device_id={"dp": peer_dp(k + 1)}, device_id_type=MESH,
        )

    for k in range(n - 1):
        z_copy(k, zm_send, zm_recv, zm_ss, zm_rs).start()

    if n > 2:
        cot_advance(2)
    for k in range(1, T):
        low_copy(k, low_send, low_recv, low_ss, low_rs).wait_recv()
    up_twice = jnp.concatenate([up, up], axis=0)
    low_spreads = []
    for g in range(G):
        low = low_send[g]
        for k in range(T - 1):
            low = low + low_recv[k, g]
        high = low.astype(BF16)
        rest = low - high.astype(F32)
        high_s = spread(high.astype(F32), g).astype(BF16)
        low_spreads.append(high_s)
        both = jnp.concatenate([high_s, spread(rest, g).astype(BF16)], axis=0)
        total = own[g, 0] + SCALE * mm(both, up_twice, TN)
        for k in range(1, H):
            x_copy(g, k).wait_recv()
            total = total + x_recv[g, k - 1].astype(F32)
        done = total.astype(BF16)
        for i in range(per):
            k = g * per + i
            z_send[k] = done[i * cap:(i + 1) * cap, :]
            if k < n - 1:
                z_copy(k, z_send, z_recv, z_ss, z_rs).start()

    for k in range(3, n):
        cot_advance(k)
    for g in range(G):
        for i in range(per):
            k = g * per + i
            col = loc_cols[k]
            pick = onehot(
                col == (lax.broadcasted_iota(jnp.int32, (cap, bal), 1) + 1).astype(F32)
            )
            cotb[g, i * cap:(i + 1) * cap, :] = mm(pick, cot_all[peer_dp(k + 1)]).astype(BF16)
        gl_send[g] = select(mm(up, cotb[g], NT), g)
    for k in range(1, T):
        low_copy(k, gl_send, gl_recv, gl_ss, gl_rs).start()

    for k in range(1, T):
        low_copy(k, gl_send, gl_recv, gl_ss, gl_rs).wait_recv()
    d_down = jnp.zeros((n * RANK, depth), F32)
    d_up = jnp.zeros((n * RANK, vw), F32)
    for g in range(G):
        gl = gl_send[g]
        for k in range(T - 1):
            gl = gl + gl_recv[k, g]
        gl_s = spread(gl.astype(BF16).astype(F32), g).astype(BF16)
        d_down = d_down + mm(gl_s, rows[g])
        d_up = d_up + mm(low_spreads[g], cotb[g])
    g_send[:, :, :depth] = (SCALE * d_down).astype(BF16).reshape(n, RANK, depth)
    g_send[:, :, depth:] = (SCALE * d_up).astype(BF16).reshape(n, RANK, vw)

    def g_copy(k):
        return pltpu.make_async_remote_copy(
            src_ref=g_send.at[peer_dp(k)], dst_ref=g_recv.at[k - 1],
            send_sem=g_ss.at[k - 1], recv_sem=g_rs.at[k - 1],
            device_id={"dp": peer_dp(k)}, device_id_type=MESH,
        )

    for k in range(1, n):
        g_copy(k).start()

    jio = (lax.broadcasted_iota(jnp.int32, (bal, cap), 0) + 1).astype(F32)
    result = mm(onehot(zm_send[n - 1][0:1] == jio), z_send[n - 1])
    for k in range(n - 1):
        z_copy(k, zm_send, zm_recv, zm_ss, zm_rs).wait_recv()
        z_copy(k, z_send, z_recv, z_ss, z_rs).wait_recv()
        result = result + mm(onehot(zm_recv[k][0:1] == jio), z_recv[k])
    out_ref[...] = result.astype(BF16)

    total = g_send[me].astype(F32)
    for k in range(1, n):
        g_copy(k).wait_recv()
        total = total + g_recv[k - 1].astype(F32)
    down_out[...] = total[:, :depth]
    up_out[...] = total[:, depth:]

    for k in range(1, n):
        fac_finish(k, True)
        cot_finish(k, True)
        g_copy(k).wait_send()
        z_copy(k - 1, zm_send, zm_recv, zm_ss, zm_rs).wait_send()
        z_copy(k - 1, z_send, z_recv, z_ss, z_rs).wait_send()
    for g in range(G):
        sib_copy(g).wait_send()
        for k in range(1, H):
            x_copy(g, k).wait_send()
    for k in range(1, T):
        low_copy(k, low_send, low_recv, low_ss, low_rs).wait_send()
        low_copy(k, gl_send, gl_recv, gl_ss, gl_rs).wait_send()


def body(n, T, tokens, weight, down, up, slot_adapter, owner_slot, balanced, cotangent):
    slots, depth = tokens.shape
    bal, vw = cotangent.shape
    adapters = owner_slot.shape[0]
    cap = -(-(slots // n) // 16) * 16
    G = 4 if n % 4 == 0 else n
    chunk = n // G * cap
    H = T // 2
    vmem, hbm = pl.BlockSpec(memory_space=pltpu.VMEM), pl.BlockSpec(memory_space=pltpu.HBM)
    dma = pltpu.SemaphoreType.DMA
    projected, grad_down, grad_up = pl.pallas_call(
        functools.partial(kernel, n, T, G, adapters),
        out_shape=(
            jax.ShapeDtypeStruct((bal, vw), BF16),
            jax.ShapeDtypeStruct((RANK, depth), F32),
            jax.ShapeDtypeStruct((RANK, vw), F32),
        ),
        in_specs=[hbm] * 8,
        out_specs=(vmem, vmem, vmem),
        scratch_shapes=[
            pltpu.SMEM((adapters,), jnp.int32),
            pltpu.VMEM((slots // 128, 128), jnp.int32),
            pltpu.VMEM((slots // 128, 128), jnp.int32),
            pltpu.VMEM((slots, depth), BF16),
            pltpu.VMEM((T, depth, vw), BF16),
            pltpu.VMEM((G, chunk, depth), BF16),
            pltpu.VMEM((n, RANK, depth + vw), BF16),
            pltpu.VMEM((n, bal, vw), BF16),
            pltpu.VMEM((G, chunk, vw), BF16),
            pltpu.VMEM((G, H, chunk, vw), BF16),
            pltpu.VMEM((G, H, chunk, vw), BF16),
            pltpu.VMEM((G, H, chunk, vw), F32),
            pltpu.VMEM((G, H - 1, chunk, vw), BF16),
            pltpu.VMEM((G, H - 1, chunk, vw), BF16),
            pltpu.VMEM((G, RANK, chunk), F32),
            pltpu.VMEM((T - 1, G, RANK, chunk), F32),
            pltpu.VMEM((G, RANK, chunk), F32),
            pltpu.VMEM((T - 1, G, RANK, chunk), F32),
            pltpu.VMEM((n, cap, vw), BF16),
            pltpu.VMEM((n, cap, vw), BF16),
            pltpu.VMEM((n, 8, cap), F32),
            pltpu.VMEM((n, 8, cap), F32),
            pltpu.VMEM((n, RANK, depth + vw), BF16),
            pltpu.VMEM((n, RANK, depth + vw), BF16),
            dma((6,)),
            dma((T + 1,)),
            dma((2, n - 1)), dma((2, n - 1)), dma((2, n - 1)), dma((2, n - 1)),
            dma((G,)), dma((G,)), dma((G, H - 1)), dma((G, H - 1)),
            dma((T - 1,)), dma((T - 1,)), dma((T - 1,)), dma((T - 1,)),
            dma((n - 1,)), dma((n - 1,)), dma((n - 1,)), dma((n - 1,)),
            dma((n - 1,)), dma((n - 1,)),
        ],
        compiler_params=pltpu.CompilerParams(
            collective_id=0, has_side_effects=True, vmem_limit_bytes=60 * 1024 * 1024
        ),
        name="value_lora",
    )(
        owner_slot, tokens, weight, down.T, up.T,
        slot_adapter.reshape(-1, 128), balanced.reshape(-1, 128), cotangent,
    )
    return projected, grad_down.T, grad_up.T


def solution(mesh):
    rows = ("groups", "dp")
    return jax.shard_map(
        functools.partial(body, mesh.shape["dp"], mesh.shape["tensor"]),
        mesh=mesh,
        in_specs=(
            P(rows, "tensor"), P("tensor", None), P("tensor", rows), P("tensor", rows),
            P(rows), P("groups"), P(rows), P(rows, "tensor"),
        ),
        out_specs=(P(rows, "tensor"), P("tensor", rows), P("tensor", rows)),
        check_vma=False,
    )
```
